32 devices in a mesh: groups: 2 (over y), seq: 4 (over z), mp: 4 (over x, core).
Axes of the slice: x: 2, y: 2, z: 4, core: 2. Of those that a mesh axis runs over, the one named last changes fastest.
Arguments:
- hidden_prompt: bfloat16 [2048, 5120], P(('groups', 'seq'), 'mp'), parts along dimension 0, may hold values from -40 to 40
- hidden_comp: bfloat16 [1024, 5120], P(('groups', 'seq'), 'mp'), parts along dimension 0, may hold values from -40 to 40
- w_query: bfloat16 [5120, 5120], P(None, 'mp'), may hold values from -0.078125 to 0.078125
- w_key: bfloat16 [5120, 1024], P(None, 'mp'), may hold values from -0.078125 to 0.078125
- w_value: bfloat16 [5120, 1024], P(None, 'mp'), may hold values from -0.078125 to 0.078125
- lengths: int32 [32], P('groups'), parts along dimension 0, may hold values from 1 to 256, 512 in all
- row_owner: int32 [1024, 1], P(('groups', 'seq')), parts along dimension 0, may hold values from 0 to 3; in each aligned block of 128 rows (0 to 127, 128 to 255, ...) at most 64 rows name the same one
Outputs:
- prompt_out: bfloat16 [2048, 5120], P(('groups', 'seq'), 'mp'), parts along dimension 0
- comp_out: bfloat16 [2048, 5120], P(('groups', 'seq'), 'mp'), parts along dimension 0
The draws below stay inside these ranges and needn't reach their ends.
There are 2 independent parts, one for each index of `groups`. The reference program is written for one: setup_inputs(seed, part) draws one part's arguments, and reference() takes and returns one part's arrays. A program takes and returns all parts, laid end to end along the dimension named above; an argument that names none is the same for every part. Nothing has to cross between parts.
Inputs may be any that keep to these rules, and one draw needn't show every extreme that they name: The lengths sum to 512, and the largest is exactly 256. `row_owner`: in every aligned block of 128 rows no owner is named more than 64 times, and in some blocks one owner is named exactly 64 times.
All inputs are finite; a program needn't handle non-finite values.
Results may differ from the reference program's by a relative error of at most 0.0072.
Values may be sent and summed in bfloat16 or wider, within the bound.
A program may use at most 128 MiB of HBM per device.

```python
import math
import jax
import jax.numpy as jnp
import numpy as np
from jax import lax

D = 5120
HEADS = 40
KV_HEADS = 8
HD = 128
CROWS = 128
NCOMP = 16
PROMPT = 1024
CTOK = 512
LMAX = 256
CAP = 64
N_SEQ = 4


def draw_hidden_prompt(key, part):
    key = jax.random.fold_in(key, 11)
    rows_key = jax.random.fold_in(key, 0)
    values = jnp.clip(jax.random.normal(rows_key, (PROMPT, D), jnp.float32), -4.0, 4.0)
    return values.astype(jnp.bfloat16)


def draw_hidden_comp(key, part):
    key = jax.random.fold_in(key, 23)
    rows_key = jax.random.fold_in(key, 0)
    values = jnp.clip(jax.random.normal(rows_key, (CTOK, D), jnp.float32), -4.0, 4.0)
    return values.astype(jnp.bfloat16)


def block_scale(rng, shape, shards, low, top_value):
    def one(position, blocks):
        heights = jax.random.uniform(jax.random.fold_in(jax.random.fold_in(rng, 6), position), (blocks,), jnp.float32, low / len(shards), top_value / len(shards))
        return jnp.repeat(jnp.exp(heights), shape[position] // blocks).reshape((-1,) + (1,) * (len(shape) - position - 1))

    gain = one(*shards[0])
    for cut in shards[1:]:
        gain = gain * one(*cut)
    return gain


def split_up(count, total, reach, lean):
    loads = [(1 << 20) // math.isqrt(standing ** lean) + 1 for standing in range(2, count + 1)]
    surplus, counts = total - reach - (count - 1), [1] * (count - 1)
    while surplus > 0:
        free = [i for i in range(count - 1) if counts[i] < reach]
        pool, left = sum([loads[i] for i in free]), surplus
        for i in free:
            extra = min(reach - counts[i], max(1, left * loads[i] // pool), surplus)
            counts[i] = counts[i] + extra
            surplus = surplus - extra
    return np.array([reach] + counts)


def ragged(stream_key, number_of, total, reach, skew):
    if number_of == 2:
        one = jax.random.randint(stream_key, (), max(1, total - reach), min(reach, total - 1) + 1)
        return jnp.stack([one, total - one])
    sizes = jnp.asarray(split_up(number_of, total, reach, skew), jnp.int32)
    twos = (number_of - 1) // 2
    giver, sink = sizes[1:1 + 2 * twos:2], sizes[2:2 + 2 * twos:2]
    margin = jnp.minimum(giver - 1, reach - sink)
    passed = jax.random.randint(jax.random.fold_in(stream_key, 1), (twos,), 0, 1 << 20) % (margin + 1)
    sizes = sizes.at[1:1 + 2 * twos:2].set(giver - passed).at[2:2 + 2 * twos:2].set(sink + passed)
    return sizes[jax.random.permutation(jax.random.fold_in(stream_key, 2), number_of)]


def shared_out(rng, own, number, rows, number_of, top, limit, lean):
    order = jax.random.permutation(rng, number_of)
    packed, common = load_shares(number_of, rows * top, limit, lean, True), load_shares(number_of, rows * top, limit, lean, False)
    places = jnp.arange(number_of)

    def named(sizes, turn):
        used = int((sizes > 0).sum())
        fixed = max(1, used // 4)
        shifted = fixed + (places - fixed + turn * (used - fixed)) % max(1, number_of - fixed)
        return jnp.zeros((number_of,), jnp.int32).at[order[jnp.where(places < fixed, places, shifted)]].set(jnp.asarray(sizes, jnp.int32))

    sizes = jnp.where(number % 4 == 0, named(packed, number // 4), named(common, number - number // 4 - 1))
    mixed = jax.random.permutation(jax.random.fold_in(own, 3), number_of)
    source_of, taker = mixed[0:number_of // 2 * 2:2], mixed[1:number_of // 2 * 2:2]
    margin = jnp.minimum(sizes[source_of] - 1, limit - sizes[taker]) // 2
    margin = jnp.where((source_of == order[0]) | (taker == order[0]) | (sizes[taker] == 0), 0, jnp.maximum(margin, 0))
    shifted = jax.random.randint(jax.random.fold_in(own, 4), (number_of // 2,), 0, 1 << 20) % (margin + 1)
    sizes = sizes.at[source_of].add(-shifted).at[taker].add(shifted)
    members = jnp.searchsorted(jnp.cumsum(sizes), jnp.arange(rows * top), side="right").astype(jnp.int32)
    grid = members.reshape(top, rows).T
    grid = grid[jax.random.permutation(jax.random.fold_in(own, 1), rows)]
    turn = jax.random.randint(jax.random.fold_in(own, 2), (rows, 1), 0, top)
    return jnp.take_along_axis(grid, (jnp.arange(top)[None, :] + turn) % top, axis=1)


def load_shares(amount, total, reach, skew, full):
    loads = [(1 << 20) // math.isqrt(grade ** skew) + 1 for grade in range(1, amount + 1)]
    largest = reach if full else min(reach, max(-(-total // amount), total * loads[0] // sum(loads)))
    least = 1 if total - largest >= amount - 1 else 0
    holding, spare = [largest] + [least] * (amount - 1), total - largest - least * (amount - 1)
    while spare > 0:
        movable = [i for i in range(1, amount) if holding[i] < largest] or [i for i in range(1, amount) if holding[i] < reach]
        mass, budget = sum([loads[i] for i in movable]), spare
        for i in movable:
            extra = min(reach - holding[i], max(1, budget * loads[i] // mass), spare)
            holding[i] = holding[i] + extra
            spare = spare - extra
    return np.array(holding)


def bell_draw(rng, extent, spread, limit, shards=(), kind=jnp.bfloat16):
    gain = block_scale(rng, extent, shards, -0.22, 0.18) if shards else 1.0
    values = jax.random.normal(rng, extent, jnp.float32) * spread * gain
    return jnp.minimum(jnp.maximum(values, -limit), limit).astype(kind)


def setup_inputs(seed: int = 0, part: int = 0) -> dict:
    streams_of = jax.random.split(jax.random.key(seed), 8)
    part_splits = jax.random.split(jax.random.fold_in(streams_of[7], part), 8)
    hidden_prompt = draw_hidden_prompt(jax.random.fold_in(jax.random.fold_in(streams_of[7], part), 71), part)
    hidden_comp = draw_hidden_comp(jax.random.fold_in(jax.random.fold_in(streams_of[7], part), 71), part)
    w_query = bell_draw(streams_of[2], (D, HEADS * HD), D ** -0.5, 0.078125, ((1, 4),))
    w_key = bell_draw(streams_of[3], (D, KV_HEADS * HD), D ** -0.5, 0.078125, ((1, 4),))
    w_value = bell_draw(streams_of[4], (D, KV_HEADS * HD), D ** -0.5, 0.078125, ((1, 4),))
    lengths = ragged(part_splits[5], NCOMP, CTOK, LMAX, 2).astype(jnp.int32)
    row_owner_keys = jax.random.split(jax.random.fold_in(part_splits[6], 1), CTOK // CROWS)
    row_owner_turns = jax.random.permutation(jax.random.fold_in(part_splits[6], 3), CTOK // CROWS)
    row_owner = jax.vmap(lambda own, number: shared_out(jax.random.fold_in(part_splits[6], 2), own, number, CROWS, N_SEQ, 1, CAP, 2))(row_owner_keys, row_owner_turns).reshape((CTOK, 1))
    return {"hidden_prompt": hidden_prompt, "hidden_comp": hidden_comp, "w_query": w_query, "w_key": w_key, "w_value": w_value, "lengths": lengths, "row_owner": row_owner}


rope_base = 1000000.0


def rotate(matrix_in, positions):
    row_count = matrix_in.shape[0]
    head_count = matrix_in.shape[1] // HD
    half_size = HD // 2
    inverse_freq = rope_base ** (-2.0 * jnp.arange(half_size, dtype=jnp.float32) / HD)
    angles = positions.astype(jnp.float32)[:, None] * inverse_freq[None, :]
    cosine = jnp.cos(angles)[:, None, :]
    sine_part = jnp.sin(angles)[:, None, :]
    shaped = matrix_in.reshape(row_count, head_count, HD)
    front_half = shaped[..., :half_size]
    back_half = shaped[..., half_size:]
    rotated = jnp.concatenate([front_half * cosine - back_half * sine_part, back_half * cosine + front_half * sine_part], -1)
    return rotated.reshape(row_count, head_count * HD)


def project(hidden, weight, positions, with_rope):
    product = jnp.dot(hidden, weight, preferred_element_type=jnp.float32)
    if with_rope:
        product = rotate(product, positions)
    return product.astype(jnp.bfloat16)


def attend(queries, key_rows, value_rows, allowed):
    row_count = queries.shape[0]
    head_count = queries.shape[1] // HD
    kv_count = key_rows.shape[1] // HD
    group_size = head_count // kv_count
    query_heads = queries.reshape(row_count, head_count, HD).transpose(1, 0, 2)
    key_heads = key_rows.reshape(-1, kv_count, HD).transpose(1, 0, 2)
    value_heads = value_rows.reshape(-1, kv_count, HD).transpose(1, 0, 2)

    def single_head(inputs_one):
        query_head, head_index = inputs_one
        key_head = lax.dynamic_index_in_dim(key_heads, head_index // group_size, 0, keepdims=False)
        value_head = lax.dynamic_index_in_dim(value_heads, head_index // group_size, 0, keepdims=False)
        scores = jnp.dot(query_head, key_head.T, preferred_element_type=jnp.float32) * (HD ** -0.5)
        scores = jnp.where(allowed, scores, -jnp.inf)
        row_max = jnp.max(scores, 1, keepdims=True)
        weights = jnp.exp(scores - row_max)
        row_total = jnp.sum(weights, 1, keepdims=True)
        mixed = jnp.dot(weights.astype(jnp.bfloat16), value_head, preferred_element_type=jnp.float32)
        return (mixed / row_total).astype(jnp.bfloat16)

    outputs = lax.map(single_head, (query_heads, jnp.arange(head_count, dtype=jnp.int32)))
    return outputs.transpose(1, 0, 2).reshape(row_count, head_count * HD)


def completion_starts(lengths, row_index):
    comp_ends = jnp.cumsum(lengths).astype(jnp.int32)
    preceding = comp_ends[None, :] <= row_index[:, None]
    return jnp.sum(jnp.where(preceding, lengths[None, :], 0), 1).astype(jnp.int32)


def owner_rank(owners, owner_count):
    chosen = (owners[:, None] == jnp.arange(owner_count, dtype=jnp.int32)[None, :]).astype(jnp.int32)
    earlier = (jnp.cumsum(chosen, 0).astype(jnp.int32) - chosen)
    return jnp.sum(earlier * chosen, 1).astype(jnp.int32)


def reference(hidden_prompt, hidden_comp, w_query, w_key, w_value, lengths, row_owner):
    prompt_rows = hidden_prompt.shape[0]
    comp_rows = hidden_comp.shape[0]
    prompt_pos = jnp.arange(prompt_rows, dtype=jnp.int32)
    comp_index = jnp.arange(comp_rows, dtype=jnp.int32)
    starts = completion_starts(lengths, comp_index)
    comp_pos = (prompt_rows + comp_index - starts).astype(jnp.int32)
    query_prompt = project(hidden_prompt, w_query, prompt_pos, True)
    key_prompt = project(hidden_prompt, w_key, prompt_pos, True)
    value_prompt = project(hidden_prompt, w_value, prompt_pos, False)
    query_comp = project(hidden_comp, w_query, comp_pos, True)
    key_comp = project(hidden_comp, w_key, comp_pos, True)
    value_comp = project(hidden_comp, w_value, comp_pos, False)
    prompt_out = attend(query_prompt, key_prompt, value_prompt, prompt_pos[None, :] <= prompt_pos[:, None])
    key_rows = jnp.concatenate([key_prompt, key_comp], 0)
    value_rows = jnp.concatenate([value_prompt, value_comp], 0)
    own_keys = (comp_index[None, :] >= starts[:, None]) & (comp_index[None, :] <= comp_index[:, None])
    allowed = jnp.concatenate([jnp.ones((comp_rows, prompt_rows), bool), own_keys], 1)
    attended = attend(query_comp, key_rows, value_rows, allowed)
    owners = row_owner[:, 0].astype(jnp.int32)
    ranks = jax.vmap(lambda block: owner_rank(block, N_SEQ))(owners.reshape(N_SEQ, CROWS)).reshape(-1)
    source_block = comp_index // CROWS
    target = (owners * (N_SEQ * CAP) + source_block * CAP + ranks).astype(jnp.int32)
    comp_out = jnp.zeros((N_SEQ * N_SEQ * CAP, attended.shape[1]), jnp.bfloat16).at[target].set(attended)
    return prompt_out, comp_out
```

```python
import functools
import math

import jax
import jax.numpy as jnp
import numpy as np
from jax import lax
from jax.experimental import pallas as pl
from jax.experimental.pallas import tpu as pltpu
from jax.sharding import PartitionSpec as P

HD = 128
HALF = HD // 2
LONGEST = 256
ROPE_BASE = 1000000.0
MESH = pl.DeviceIdType.MESH
BF16 = jnp.bfloat16
F32 = jnp.float32
NEG = -1e30


def dot(a, b):
    return jnp.dot(a, b, preferred_element_type=F32)


def dot_t(a, b):
    return lax.dot_general(a, b, (((1,), (1,)), ((), ())), preferred_element_type=F32)


def kernel(
    cfg,
    hp_ref, hc_ref, wq_ref, wk_ref, wv_ref, len_ref, own_ref, freq_ref,
    po_ref, co_ref,
    hid, wq, wk, wv, cosb, sinb, qb, kv, ckv, scat, sendb,
    w_sem, own_sem, x_send, x_recv, f_send, zr_send, zr_recv, zl_send, zl_recv,
    c_send, c_recv, a_send, a_recv,
):
    n_mp, n_seq, prows, crows, feat, qcols, kcols, ncomp = cfg
    nheads, nkv = qcols // HD, kcols // HD
    group = nheads // nkv
    cap = 2 * crows // n_seq
    chunk = crows
    npc = prows // chunk
    nchunk = npc + 1
    back = min(-(-(LONGEST - 1) // crows), n_seq - 1)
    s = lax.axis_index("seq")
    m = lax.axis_index("mp")
    core = lax.rem(m, 2)
    sib = m + 1 - 2 * core
    nx = n_mp // 2

    def peer(k):
        return lax.rem(m + 2 * k, n_mp)

    def seq_at(k):
        return lax.rem(s + k + n_seq, n_seq)

    barrier = pltpu.get_barrier_semaphore()
    pl.semaphore_signal(barrier, inc=1, device_id={"mp": sib}, device_id_type=MESH)
    for k in range(1, nx):
        pl.semaphore_signal(barrier, inc=1, device_id={"mp": peer(k)}, device_id_type=MESH)
    for k in range(1, n_seq):
        pl.semaphore_signal(barrier, inc=1, device_id={"seq": seq_at(k)}, device_id_type=MESH)

    def rows_of(c):
        return pl.ds(c * chunk, chunk)

    def source(c):
        return hp_ref.at[rows_of(c)] if c < npc else hc_ref

    own_copies = [
        pltpu.make_async_copy(source(c), hid.at[m, rows_of(c)], own_sem.at[c]) for c in range(nchunk)
    ]
    for copy in own_copies:
        copy.start()
    w_copies = [
        pltpu.make_async_copy(wk_ref, wk, w_sem.at[0]),
        pltpu.make_async_copy(wv_ref, wv, w_sem.at[1]),
        pltpu.make_async_copy(wq_ref, wq, w_sem.at[2]),
    ]

    pl.semaphore_wait(barrier, n_seq + nx - 1)

    def x_copy(c, k):
        target = sib if k == 0 else peer(k)
        return pltpu.make_async_remote_copy(
            src_ref=source(c), dst_ref=hid.at[m, rows_of(c)],
            send_sem=x_send.at[c, k], recv_sem=x_recv.at[c, k],
            device_id={"mp": target}, device_id_type=MESH,
        )

    def f_copy(c, k):
        held = lax.rem(m - 2 * k + 2 * n_mp, n_mp)
        return pltpu.make_async_remote_copy(
            src_ref=hid.at[held, rows_of(c)], dst_ref=hid.at[held, rows_of(c)],
            send_sem=f_send.at[c, k - 1], recv_sem=x_recv.at[c, nx - 1 + k],
            device_id={"mp": sib}, device_id_type=MESH,
        )

    for c in range(nchunk):
        for k in list(range(1, nx)) + [0]:
            x_copy(c, k).start()
    for copy in w_copies:
        copy.start()

    ii = lax.broadcasted_iota(jnp.int32, (ncomp, ncomp), 0)
    jj = lax.broadcasted_iota(jnp.int32, (ncomp, ncomp), 1)
    lens = jnp.broadcast_to(len_ref[...], (ncomp, ncomp))
    ends_col = jnp.sum(jnp.where(jj <= ii, lens, 0), 1, keepdims=True)
    ends_row = jnp.sum(jnp.where(ii == jj, jnp.broadcast_to(ends_col, (ncomp, ncomp)), 0), 0, keepdims=True)
    crow = s * crows + lax.broadcasted_iota(jnp.int32, (crows, 1), 0)
    ends_all = jnp.broadcast_to(ends_row, (crows, ncomp))
    starts = jnp.max(jnp.where(ends_all <= crow, ends_all, 0), 1, keepdims=True)
    freq = freq_ref[...]
    sign = jnp.where(lax.broadcasted_iota(jnp.int32, (1, HD), 1) < HALF, -1.0, 1.0)
    for c in range(nchunk):
        if c < npc:
            pos = s * prows + c * chunk + lax.broadcasted_iota(jnp.int32, (chunk, 1), 0)
        else:
            pos = n_seq * prows + crow - starts
        angle = pos.astype(F32) * freq
        cosb[rows_of(c)] = jnp.cos(angle)
        sinb[rows_of(c)] = jnp.sin(angle) * sign

    ri = lax.broadcasted_iota(jnp.int32, (crows, crows), 0)
    rj = lax.broadcasted_iota(jnp.int32, (crows, crows), 1)
    own_i = jnp.broadcast_to(own_ref[...], (crows, crows))
    own_row = jnp.sum(jnp.where(ri == rj, own_i, 0), 0, keepdims=True)
    earlier = jnp.where((own_i == own_row) & (ri < rj), 1, 0)
    slot_row = own_row * cap + jnp.sum(earlier, 0, keepdims=True)
    slots = lax.broadcasted_iota(jnp.int32, (n_seq * cap, crows), 0)
    scat[...] = jnp.where(slots == slot_row, 1.0, 0.0).astype(BF16)

    def zr_copy(c, d):
        t = lax.rem(s - d + 1 + n_seq, n_seq)
        return pltpu.make_async_remote_copy(
            src_ref=kv.at[t, rows_of(c)], dst_ref=kv.at[t, rows_of(c)],
            send_sem=zr_send.at[c, d - 1], recv_sem=zr_recv.at[c, d - 1],
            device_id={"seq": seq_at(1)}, device_id_type=MESH,
        )

    def zl_copy(c, d):
        t = lax.rem(s + d - 1, n_seq)
        return pltpu.make_async_remote_copy(
            src_ref=kv.at[t, rows_of(c)], dst_ref=kv.at[t, rows_of(c)],
            send_sem=zl_send.at[c, d - 1], recv_sem=zl_recv.at[c, d - 1],
            device_id={"seq": seq_at(-1)}, device_id_type=MESH,
        )

    def zr_in(c, d):
        t = lax.rem(s - d + n_seq, n_seq)
        return pltpu.make_async_remote_copy(
            src_ref=kv.at[t, rows_of(c)], dst_ref=kv.at[t, rows_of(c)],
            send_sem=zr_send.at[c, d - 1], recv_sem=zr_recv.at[c, d - 1],
            device_id={"seq": seq_at(1)}, device_id_type=MESH,
        )

    def zl_in(c, d):
        t = lax.rem(s + d, n_seq)
        return pltpu.make_async_remote_copy(
            src_ref=kv.at[t, rows_of(c)], dst_ref=kv.at[t, rows_of(c)],
            send_sem=zl_send.at[c, d - 1], recv_sem=zl_recv.at[c, d - 1],
            device_id={"seq": seq_at(-1)}, device_id_type=MESH,
        )

    def z_first(c):
        @pl.when(s < n_seq - 1)
        def _():
            zr_copy(c, 1).start()

        @pl.when(s > 0)
        def _():
            zl_copy(c, 1).start()

    def z_step(c, d):
        @pl.when(s >= d)
        def _():
            zr_in(c, d).wait_recv()

            if d < n_seq - 1:
                @pl.when(s < n_seq - 1)
                def _():
                    zr_copy(c, d + 1).start()

        @pl.when(s + d < n_seq)
        def _():
            zl_in(c, d).wait_recv()

            if d < n_seq - 1:
                @pl.when(s > 0)
                def _():
                    zl_copy(c, d + 1).start()

    def c_copy(d):
        return pltpu.make_async_remote_copy(
            src_ref=ckv.at[back], dst_ref=ckv.at[back - d],
            send_sem=c_send.at[d - 1], recv_sem=c_recv.at[d - 1],
            device_id={"seq": seq_at(d)}, device_id_type=MESH,
        )

    for d in range(1, back + 1):
        @pl.when(s < d)
        def _():
            ckv[back - d] = jnp.zeros((crows, 2 * kcols), BF16)

    def product(c, weight, cols):
        total = None
        for q in range(n_mp):
            part = dot(hid[q, c * chunk:(c + 1) * chunk, :], weight[q * feat:(q + 1) * feat, cols])
            total = part if total is None else total + part
        return total

    def rope(x, c):
        cos = cosb[c * chunk:(c + 1) * chunk, :]
        sin = sinb[c * chunk:(c + 1) * chunk, :]
        return (x * cos + pltpu.roll(x, HALF, 1) * sin).astype(BF16)

    kw = kcols
    qw = 2 * HD if nheads % 2 == 0 else HD

    for c in range(nchunk):
        own_copies[c].wait()
        for k in range(1, nx):
            x_copy(c, k).wait_recv()
            f_copy(c, k).start()
        x_copy(c, 0).wait_recv()
        for k in range(1, nx):
            f_copy(c, k).wait_recv()
        if c == 0:
            w_copies[0].wait()
            w_copies[1].wait()
        kp = product(c, wk, slice(None))
        keys = [rope(kp[:, h * HD:(h + 1) * HD], c) for h in range(nkv)]
        vals = product(c, wv, slice(None)).astype(BF16)
        if c < npc:
            for h in range(nkv):
                kv[s, c * chunk:(c + 1) * chunk, h * HD:(h + 1) * HD] = keys[h]
            kv[s, c * chunk:(c + 1) * chunk, kcols:] = vals
            z_first(c)
        else:
            for h in range(nkv):
                ckv[back, :, h * HD:(h + 1) * HD] = keys[h]
            ckv[back, :, kcols:] = vals
            for d in range(1, back + 1):
                @pl.when(s + d < n_seq)
                def _():
                    c_copy(d).start()
        if c == 0:
            w_copies[2].wait()

        def q_tile(t, carry):
            qp = product(c, wq, pl.ds(pl.multiple_of(t * qw, qw), qw))
            for h in range(qw // HD):
                qb[t * (qw // HD) + h, c * chunk:(c + 1) * chunk, :] = rope(qp[:, h * HD:(h + 1) * HD], c)
            return carry

        lax.fori_loop(0, qcols // qw, q_tile, 0)
        if c < npc:
            z_step(c, 1)
        if c >= 1:
            for d in range(2, n_seq):
                z_step(c - 1, d)

    scale = HD ** -0.5 * math.log2(math.e)
    total_keys = n_seq * prows

    for d in range(1, back + 1):
        @pl.when(s >= d)
        def _():
            c_copy(d).wait_recv()

    nck = (back + 1) * crows
    ckey = (s - back) * crows + lax.broadcasted_iota(jnp.int32, (crows, nck), 1)
    cmask = jnp.where((ckey >= starts) & (ckey <= crow), 0.0, NEG)

    def a_copy(g, k):
        o = seq_at(k)
        return pltpu.make_async_remote_copy(
            src_ref=sendb.at[g, pl.ds(pl.multiple_of(o * cap, cap), cap)],
            dst_ref=co_ref.at[pl.ds(pl.multiple_of(s * cap, cap), cap), pl.ds(g * group * HD, group * HD)],
            send_sem=a_send.at[g, k - 1], recv_sem=a_recv.at[g, k - 1],
            device_id={"seq": o}, device_id_type=MESH,
        )

    def a_in(g, k):
        o = seq_at(-k)
        return pltpu.make_async_remote_copy(
            src_ref=sendb.at[g, pl.ds(pl.multiple_of(o * cap, cap), cap)],
            dst_ref=co_ref.at[pl.ds(pl.multiple_of(o * cap, cap), cap), pl.ds(g * group * HD, group * HD)],
            send_sem=a_send.at[g, k - 1], recv_sem=a_recv.at[g, k - 1],
            device_id={"seq": o}, device_id_type=MESH,
        )

    for g in range(nkv):
        kcol = slice(g * HD, (g + 1) * HD)
        vcol = slice(kcols + g * HD, kcols + (g + 1) * HD)
        for h in range(group):
            q = qb[g * group + h, npc * chunk:(npc + 1) * chunk, :]
            sp = dot_t(q, kv[:, :, kcol].reshape(total_keys, HD)) * scale
            sc = dot_t(q, ckv[:, :, kcol].reshape(nck, HD)) * scale + cmask
            top = jnp.maximum(jnp.max(sp, 1, keepdims=True), jnp.max(sc, 1, keepdims=True))
            ep = jnp.exp2(sp - top)
            ec = jnp.exp2(sc - top)
            total = jnp.sum(ep, 1, keepdims=True) + jnp.sum(ec, 1, keepdims=True)
            mixed = dot(ep.astype(BF16), kv[:, :, vcol].reshape(total_keys, HD))
            mixed = mixed + dot(ec.astype(BF16), ckv[:, :, vcol].reshape(nck, HD))
            out = (mixed / total).astype(BF16)
            sendb[g, :, h * HD:(h + 1) * HD] = dot(scat[...], out).astype(BF16)
        for k in range(1, n_seq):
            a_copy(g, k).start()
        mine = pl.ds(pl.multiple_of(s * cap, cap), cap)
        co_ref[mine, g * group * HD:(g + 1) * group * HD] = sendb[g, mine, :]

    ppos = s * prows + lax.broadcasted_iota(jnp.int32, (prows, 1), 0)
    pkey = lax.broadcasted_iota(jnp.int32, (prows, total_keys), 1)
    for g in range(nkv):
        kcol = slice(g * HD, (g + 1) * HD)
        vcol = slice(kcols + g * HD, kcols + (g + 1) * HD)
        for h in range(group):
            head = g * group + h
            q = qb[head, :prows, :]
            sp = dot_t(q, kv[:, :, kcol].reshape(total_keys, HD)) * scale
            sp = jnp.where(pkey <= ppos, sp, NEG)
            top = jnp.max(sp, 1, keepdims=True)
            ep = jnp.exp2(sp - top)
            total = jnp.sum(ep, 1, keepdims=True)
            mixed = dot(ep.astype(BF16), kv[:, :, vcol].reshape(total_keys, HD))
            po_ref[:, head * HD:(head + 1) * HD] = (mixed / total).astype(BF16)

    for g in range(nkv):
        for k in range(1, n_seq):
            a_in(g, k).wait_recv()
    for g in range(nkv):
        for k in range(1, n_seq):
            a_copy(g, k).wait_send()
    for c in range(nchunk):
        for k in range(nx):
            x_copy(c, k).wait_send()
        for k in range(1, nx):
            f_copy(c, k).wait_send()
    for c in range(npc):
        for d in range(1, n_seq):
            @pl.when((s - d + 1 >= 0) & (s < n_seq - 1))
            def _():
                zr_copy(c, d).wait_send()

            @pl.when((s + d - 1 < n_seq) & (s > 0))
            def _():
                zl_copy(c, d).wait_send()
    for d in range(1, back + 1):
        @pl.when(s + d < n_seq)
        def _():
            c_copy(d).wait_send()


def local(n_mp, n_seq, hidden_prompt, hidden_comp, w_query, w_key, w_value, lengths, row_owner):
    prows, feat = hidden_prompt.shape
    crows = hidden_comp.shape[0]
    depth, qcols = w_query.shape
    kcols = w_key.shape[1]
    ncomp = lengths.shape[0]
    nkv = kcols // HD
    group = qcols // kcols
    cap = 2 * crows // n_seq
    npc = prows // crows
    nchunk = npc + 1
    nx = n_mp // 2
    back = min(-(-(LONGEST - 1) // crows), n_seq - 1)
    half = ROPE_BASE ** (-2.0 * np.arange(HALF, dtype=np.float64) / HD)
    freq = jnp.asarray(np.concatenate([half, half])[None, :], F32)
    cfg = (n_mp, n_seq, prows, crows, feat, qcols, kcols, ncomp)
    hbm = pl.BlockSpec(memory_space=pl.ANY)
    vmem = pl.BlockSpec(memory_space=pltpu.VMEM)
    dma = lambda *shape: pltpu.SemaphoreType.DMA(shape)
    rows = prows + crows
    z_hops = max(n_seq - 1, 1)
    return pl.pallas_call(
        functools.partial(kernel, cfg),
        out_shape=(
            jax.ShapeDtypeStruct((prows, qcols), BF16),
            jax.ShapeDtypeStruct((n_seq * cap, qcols), BF16),
        ),
        in_specs=[hbm] * 5 + [vmem] * 3,
        out_specs=(vmem, vmem),
        scratch_shapes=[
            pltpu.VMEM((n_mp, rows, feat), BF16),
            pltpu.VMEM((depth, qcols), BF16),
            pltpu.VMEM((depth, kcols), BF16),
            pltpu.VMEM((depth, kcols), BF16),
            pltpu.VMEM((rows, HD), F32),
            pltpu.VMEM((rows, HD), F32),
            pltpu.VMEM((qcols // HD, rows, HD), BF16),
            pltpu.VMEM((n_seq, prows, 2 * kcols), BF16),
            pltpu.VMEM((back + 1, crows, 2 * kcols), BF16),
            pltpu.VMEM((n_seq * cap, crows), BF16),
            pltpu.VMEM((nkv, n_seq * cap, group * HD), BF16),
            dma(3),
            dma(nchunk),
            dma(nchunk, nx),
            dma(nchunk, 2 * nx - 1),
            dma(nchunk, nx - 1),
            dma(npc, z_hops), dma(npc, z_hops), dma(npc, z_hops), dma(npc, z_hops),
            dma(back), dma(back),
            dma(nkv, z_hops), dma(nkv, z_hops),
        ],
        compiler_params=pltpu.CompilerParams(
            collective_id=0, has_side_effects=True, vmem_limit_bytes=56 * 1024 * 1024
        ),
        cost_estimate=pl.CostEstimate(
            flops=2 * rows * depth * (qcols + 2 * kcols), bytes_accessed=2 * depth * (qcols + 2 * kcols), transcendentals=0
        ),
        name="grouped_attention",
    )(hidden_prompt, hidden_comp, w_query, w_key, w_value, lengths.reshape(1, ncomp), row_owner, freq)


def solution(mesh):
    placed = (
        P(("groups", "seq"), "mp"),
        P(("groups", "seq"), "mp"),
        P(None, "mp"),
        P(None, "mp"),
        P(None, "mp"),
        P("groups"),
        P(("groups", "seq"), None),
    )
    return jax.shard_map(
        functools.partial(local, mesh.shape["mp"], mesh.shape["seq"]),
        mesh=mesh,
        in_specs=placed,
        out_specs=(P(("groups", "seq"), "mp"), P(("groups", "seq"), "mp")),
        check_vma=False,
    )
```

```python
import functools
import math

import jax
import jax.numpy as jnp
import numpy as np
from jax import lax
from jax.experimental import pallas as pl
from jax.experimental.pallas import tpu as pltpu
from jax.sharding import PartitionSpec as P

HD = 128
HALF = HD // 2
LONGEST = 256
ROPE_BASE = 1000000.0
MESH = pl.DeviceIdType.MESH
BF16 = jnp.bfloat16
F32 = jnp.float32
NEG = -1e30
PIECES = 4


def dot(a, b):
    return jnp.dot(a, b, preferred_element_type=F32)


def dot_t(a, b):
    return lax.dot_general(a, b, (((1,), (1,)), ((), ())), preferred_element_type=F32)


def kernel(
    cfg,
    hp_ref, hc_ref, wq_ref, wk_ref, wv_ref, len_ref, own_ref, freq_ref,
    po_ref, co_ref,
    hid, wq, wk, wv, cosb, sinb, qb, kv, ckv, scat, sendb, tops, sums, mixes,
    w_sem, own_sem, x_send, x_recv, f_send, zr_send, zr_recv, zl_send, zl_recv,
    c_send, c_recv, a_send, a_recv,
):
    n_mp, n_seq, prows, crows, feat, qcols, kcols, ncomp = cfg
    nheads, nkv = qcols // HD, kcols // HD
    group = nheads // nkv
    cap = 2 * crows // n_seq
    chunk = crows
    npc = prows // chunk
    nchunk = npc + 1
    back = min(-(-(LONGEST - 1) // crows), n_seq - 1)
    s = lax.axis_index("seq")
    m = lax.axis_index("mp")
    core = lax.rem(m, 2)
    sib = m + 1 - 2 * core
    nx = n_mp // 2

    def peer(k):
        return lax.rem(m + 2 * k, n_mp)

    def seq_at(k):
        return lax.rem(s + k + n_seq, n_seq)

    barrier = pltpu.get_barrier_semaphore()
    pl.semaphore_signal(barrier, inc=1, device_id={"mp": sib}, device_id_type=MESH)
    for k in range(1, nx):
        pl.semaphore_signal(barrier, inc=1, device_id={"mp": peer(k)}, device_id_type=MESH)
    for k in range(1, n_seq):
        pl.semaphore_signal(barrier, inc=1, device_id={"seq": seq_at(k)}, device_id_type=MESH)

    def rows_of(c):
        return pl.ds(c * chunk, chunk)

    def source(c):
        return hp_ref.at[rows_of(c)] if c < npc else hc_ref

    own_copies = [
        pltpu.make_async_copy(source(c), hid.at[m, rows_of(c)], own_sem.at[c]) for c in range(nchunk)
    ]
    for copy in own_copies:
        copy.start()
    w_copies = [
        pltpu.make_async_copy(wk_ref, wk, w_sem.at[0]),
        pltpu.make_async_copy(wv_ref, wv, w_sem.at[1]),
        pltpu.make_async_copy(wq_ref, wq, w_sem.at[2]),
    ]

    pl.semaphore_wait(barrier, n_seq + nx - 1)

    def x_copy(c, k):
        target = sib if k == 0 else peer(k)
        return pltpu.make_async_remote_copy(
            src_ref=source(c), dst_ref=hid.at[m, rows_of(c)],
            send_sem=x_send.at[c, k], recv_sem=x_recv.at[c, k],
            device_id={"mp": target}, device_id_type=MESH,
        )

    def f_copy(c, k):
        held = lax.rem(m - 2 * k + 2 * n_mp, n_mp)
        return pltpu.make_async_remote_copy(
            src_ref=hid.at[held, rows_of(c)], dst_ref=hid.at[held, rows_of(c)],
            send_sem=f_send.at[c, k - 1], recv_sem=x_recv.at[c, nx - 1 + k],
            device_id={"mp": sib}, device_id_type=MESH,
        )

    for c in range(nchunk):
        for k in list(range(1, nx)) + [0]:
            x_copy(c, k).start()
    for copy in w_copies:
        copy.start()

    ii = lax.broadcasted_iota(jnp.int32, (ncomp, ncomp), 0)
    jj = lax.broadcasted_iota(jnp.int32, (ncomp, ncomp), 1)
    lens = jnp.broadcast_to(len_ref[...], (ncomp, ncomp))
    ends_col = jnp.sum(jnp.where(jj <= ii, lens, 0), 1, keepdims=True)
    ends_row = jnp.sum(jnp.where(ii == jj, jnp.broadcast_to(ends_col, (ncomp, ncomp)), 0), 0, keepdims=True)
    crow = s * crows + lax.broadcasted_iota(jnp.int32, (crows, 1), 0)
    ends_all = jnp.broadcast_to(ends_row, (crows, ncomp))
    starts = jnp.max(jnp.where(ends_all <= crow, ends_all, 0), 1, keepdims=True)
    freq = freq_ref[...]
    sign = jnp.where(lax.broadcasted_iota(jnp.int32, (1, HD), 1) < HALF, -1.0, 1.0)
    for c in range(nchunk):
        if c < npc:
            pos = s * prows + c * chunk + lax.broadcasted_iota(jnp.int32, (chunk, 1), 0)
        else:
            pos = n_seq * prows + crow - starts
        angle = pos.astype(F32) * freq
        cosb[rows_of(c)] = jnp.cos(angle)
        sinb[rows_of(c)] = jnp.sin(angle) * sign

    ri = lax.broadcasted_iota(jnp.int32, (crows, crows), 0)
    rj = lax.broadcasted_iota(jnp.int32, (crows, crows), 1)
    own_row = own_ref[...]
    own_all = jnp.broadcast_to(own_row, (crows, crows))
    own_col = jnp.sum(jnp.where(ri == rj, own_all, 0), 1, keepdims=True)
    earlier = jnp.where((own_col == own_all) & (ri < rj), 1, 0)
    slot_row = own_row * cap + jnp.sum(earlier, 0, keepdims=True)
    slots = lax.broadcasted_iota(jnp.int32, (n_seq * cap, crows), 0)
    scat[...] = jnp.where(slots == slot_row, 1.0, 0.0).astype(BF16)

    def zr_copy(c, d):
        t = lax.rem(s - d + 1 + n_seq, n_seq)
        return pltpu.make_async_remote_copy(
            src_ref=kv.at[t, rows_of(c)], dst_ref=kv.at[t, rows_of(c)],
            send_sem=zr_send.at[c, d - 1], recv_sem=zr_recv.at[c, d - 1],
            device_id={"seq": seq_at(1)}, device_id_type=MESH,
        )

    def zl_copy(c, d):
        t = lax.rem(s + d - 1, n_seq)
        return pltpu.make_async_remote_copy(
            src_ref=kv.at[t, rows_of(c)], dst_ref=kv.at[t, rows_of(c)],
            send_sem=zl_send.at[c, d - 1], recv_sem=zl_recv.at[c, d - 1],
            device_id={"seq": seq_at(-1)}, device_id_type=MESH,
        )

    def zr_in(c, d):
        t = lax.rem(s - d + n_seq, n_seq)
        return pltpu.make_async_remote_copy(
            src_ref=kv.at[t, rows_of(c)], dst_ref=kv.at[t, rows_of(c)],
            send_sem=zr_send.at[c, d - 1], recv_sem=zr_recv.at[c, d - 1],
            device_id={"seq": seq_at(1)}, device_id_type=MESH,
        )

    def zl_in(c, d):
        t = lax.rem(s + d, n_seq)
        return pltpu.make_async_remote_copy(
            src_ref=kv.at[t, rows_of(c)], dst_ref=kv.at[t, rows_of(c)],
            send_sem=zl_send.at[c, d - 1], recv_sem=zl_recv.at[c, d - 1],
            device_id={"seq": seq_at(-1)}, device_id_type=MESH,
        )

    def z_first(c):
        @pl.when(s < n_seq - 1)
        def _():
            zr_copy(c, 1).start()

        @pl.when(s > 0)
        def _():
            zl_copy(c, 1).start()

    def z_step(c, d):
        @pl.when(s >= d)
        def _():
            zr_in(c, d).wait_recv()

            if d < n_seq - 1:
                @pl.when(s < n_seq - 1)
                def _():
                    zr_copy(c, d + 1).start()

        @pl.when(s + d < n_seq)
        def _():
            zl_in(c, d).wait_recv()

            if d < n_seq - 1:
                @pl.when(s > 0)
                def _():
                    zl_copy(c, d + 1).start()

    def c_copy(d):
        return pltpu.make_async_remote_copy(
            src_ref=ckv.at[back], dst_ref=ckv.at[back - d],
            send_sem=c_send.at[d - 1], recv_sem=c_recv.at[d - 1],
            device_id={"seq": seq_at(d)}, device_id_type=MESH,
        )

    for d in range(1, back + 1):
        @pl.when(s < d)
        def _():
            ckv[back - d] = jnp.zeros((crows, 2 * kcols), BF16)

    def product(c, weight, cols):
        total = None
        for q in range(n_mp):
            part = dot(hid[q, c * chunk:(c + 1) * chunk, :], weight[q * feat:(q + 1) * feat, cols])
            total = part if total is None else total + part
        return total

    def rope(x, c):
        cos = cosb[c * chunk:(c + 1) * chunk, :]
        sin = sinb[c * chunk:(c + 1) * chunk, :]
        return (x * cos + pltpu.roll(x, HALF, 1) * sin).astype(BF16)

    kw = kcols
    qw = 2 * HD if nheads % 2 == 0 else HD

    for c in range(nchunk):
        own_copies[c].wait()
        for k in range(1, nx):
            x_copy(c, k).wait_recv()
            f_copy(c, k).start()
        x_copy(c, 0).wait_recv()
        for k in range(1, nx):
            f_copy(c, k).wait_recv()
        if c == 0:
            w_copies[0].wait()
            w_copies[1].wait()
        kp = product(c, wk, slice(None))
        keys = [rope(kp[:, h * HD:(h + 1) * HD], c) for h in range(nkv)]
        vals = product(c, wv, slice(None)).astype(BF16)
        if c < npc:
            for h in range(nkv):
                kv[s, c * chunk:(c + 1) * chunk, h * HD:(h + 1) * HD] = keys[h]
            kv[s, c * chunk:(c + 1) * chunk, kcols:] = vals
            z_first(c)
        else:
            for h in range(nkv):
                ckv[back, :, h * HD:(h + 1) * HD] = keys[h]
            ckv[back, :, kcols:] = vals
            for d in range(1, back + 1):
                @pl.when(s + d < n_seq)
                def _():
                    c_copy(d).start()
        if c == 0:
            w_copies[2].wait()

        def q_tile(t, carry):
            qp = product(c, wq, pl.ds(pl.multiple_of(t * qw, qw), qw))
            for h in range(qw // HD):
                qb[t * (qw // HD) + h, c * chunk:(c + 1) * chunk, :] = rope(qp[:, h * HD:(h + 1) * HD], c)
            return carry

        tiles = qcols // qw
        lax.fori_loop(0, tiles // 2, q_tile, 0)
        if c >= 1 and n_seq > 2:
            z_step(c - 1, 2)
        lax.fori_loop(tiles // 2, tiles, q_tile, 0)
        if c < npc:
            z_step(c, 1)

    scale = HD ** -0.5 * math.log2(math.e)
    total_keys = n_seq * prows
    early = (npc - 1) * chunk

    for c in range(npc - 1):
        for d in range(3, n_seq):
            z_step(c, d)

    def key_block(g, first, stop):
        return kv[:, first:stop, g * HD:(g + 1) * HD].reshape(n_seq * (stop - first), HD)

    def value_block(g, first, stop):
        return kv[:, first:stop, kcols + g * HD:kcols + (g + 1) * HD].reshape(n_seq * (stop - first), HD)

    for g in range(nkv):
        for h in range(group):
            head = g * group + h
            q = qb[head, npc * chunk:(npc + 1) * chunk, :]
            sp = dot_t(q, key_block(g, 0, early)) * scale
            top = jnp.max(sp, 1, keepdims=True)
            ep = jnp.exp2(sp - top)
            tops[head] = jnp.broadcast_to(top, (crows, HD))
            sums[head] = jnp.broadcast_to(jnp.sum(ep, 1, keepdims=True), (crows, HD))
            mixes[head] = dot(ep.astype(BF16), value_block(g, 0, early))

    for d in range(3, n_seq):
        z_step(npc - 1, d)
    for d in range(1, back + 1):
        @pl.when(s >= d)
        def _():
            c_copy(d).wait_recv()

    nck = (back + 1) * crows
    ckey = (s - back) * crows + lax.broadcasted_iota(jnp.int32, (crows, nck), 1)
    cmask = jnp.where((ckey >= starts) & (ckey <= crow), 0.0, NEG)

    def a_copy(g, k):
        o = seq_at(k)
        return pltpu.make_async_remote_copy(
            src_ref=sendb.at[g, pl.ds(pl.multiple_of(o * cap, cap), cap)],
            dst_ref=co_ref.at[pl.ds(pl.multiple_of(s * cap, cap), cap), pl.ds(g * group * HD, group * HD)],
            send_sem=a_send.at[g, k - 1], recv_sem=a_recv.at[g, k - 1],
            device_id={"seq": o}, device_id_type=MESH,
        )

    def a_in(g, k):
        o = seq_at(-k)
        return pltpu.make_async_remote_copy(
            src_ref=sendb.at[g, pl.ds(pl.multiple_of(o * cap, cap), cap)],
            dst_ref=co_ref.at[pl.ds(pl.multiple_of(o * cap, cap), cap), pl.ds(g * group * HD, group * HD)],
            send_sem=a_send.at[g, k - 1], recv_sem=a_recv.at[g, k - 1],
            device_id={"seq": o}, device_id_type=MESH,
        )

    for g in range(nkv):
        kcol = slice(g * HD, (g + 1) * HD)
        vcol = slice(kcols + g * HD, kcols + (g + 1) * HD)
        for h in range(group):
            head = g * group + h
            q = qb[head, npc * chunk:(npc + 1) * chunk, :]
            sp = dot_t(q, key_block(g, early, prows)) * scale
            sc = dot_t(q, ckv[:, :, kcol].reshape(nck, HD)) * scale + cmask
            before = tops[head][:, :1]
            top = jnp.maximum(jnp.max(sp, 1, keepdims=True), jnp.max(sc, 1, keepdims=True))
            top = jnp.maximum(top, before)
            ep = jnp.exp2(sp - top)
            ec = jnp.exp2(sc - top)
            shrink = jnp.exp2(before - top)
            total = jnp.sum(ep, 1, keepdims=True) + jnp.sum(ec, 1, keepdims=True) + sums[head][:, :1] * shrink
            mixed = dot(ep.astype(BF16), value_block(g, early, prows))
            mixed = mixed + dot(ec.astype(BF16), ckv[:, :, vcol].reshape(nck, HD)) + mixes[head] * shrink
            out = (mixed / total).astype(BF16)
            sendb[g, :, h * HD:(h + 1) * HD] = dot(scat[...], out).astype(BF16)
        for k in range(1, n_seq):
            a_copy(g, k).start()
        mine = pl.ds(pl.multiple_of(s * cap, cap), cap)
        co_ref[mine, g * group * HD:(g + 1) * group * HD] = sendb[g, mine, :]

    ppos = s * prows + lax.broadcasted_iota(jnp.int32, (prows, 1), 0)
    pkey = lax.broadcasted_iota(jnp.int32, (prows, total_keys), 1)
    for g in range(nkv):
        kcol = slice(g * HD, (g + 1) * HD)
        vcol = slice(kcols + g * HD, kcols + (g + 1) * HD)
        for h in range(group):
            head = g * group + h
            q = qb[head, :prows, :]
            sp = dot_t(q, kv[:, :, kcol].reshape(total_keys, HD)) * scale
            sp = jnp.where(pkey <= ppos, sp, NEG)
            top = jnp.max(sp, 1, keepdims=True)
            ep = jnp.exp2(sp - top)
            total = jnp.sum(ep, 1, keepdims=True)
            mixed = dot(ep.astype(BF16), kv[:, :, vcol].reshape(total_keys, HD))
            po_ref[:, head * HD:(head + 1) * HD] = (mixed / total).astype(BF16)

    for g in range(nkv):
        for k in range(1, n_seq):
            a_in(g, k).wait_recv()
    for g in range(nkv):
        for k in range(1, n_seq):
            a_copy(g, k).wait_send()
    for c in range(nchunk):
        for k in range(nx):
            x_copy(c, k).wait_send()
        for k in range(1, nx):
            f_copy(c, k).wait_send()
    for c in range(npc):
        for d in range(1, n_seq):
            @pl.when((s - d + 1 >= 0) & (s < n_seq - 1))
            def _():
                zr_copy(c, d).wait_send()

            @pl.when((s + d - 1 < n_seq) & (s > 0))
            def _():
                zl_copy(c, d).wait_send()
    for d in range(1, back + 1):
        @pl.when(s + d < n_seq)
        def _():
            c_copy(d).wait_send()


def hand_over(po_in, co_in, po_ref, co_ref, stage, in_sem, out_sem):
    pieces = in_sem.shape[1]
    reads, writes = [], []
    for i, (src, dst) in enumerate(((po_in, po_ref), (co_in, co_ref))):
        step = src.shape[0] // pieces
        for p in range(pieces):
            part = pl.ds(p * step, step)
            held = stage.at[i, part]
            reads.append(pltpu.make_async_copy(src.at[part], held, in_sem.at[i, p]))
            writes.append(pltpu.make_async_copy(held, dst.at[part], out_sem.at[i, p]))
    for read in reads:
        read.start()
    for read, write in zip(reads, writes):
        read.wait()
        write.start()
    for write in writes:
        write.wait()


def local(n_mp, n_seq, hidden_prompt, hidden_comp, w_query, w_key, w_value, lengths, row_owner):
    prows, feat = hidden_prompt.shape
    crows = hidden_comp.shape[0]
    depth, qcols = w_query.shape
    kcols = w_key.shape[1]
    ncomp = lengths.shape[0]
    nkv = kcols // HD
    group = qcols // kcols
    cap = 2 * crows // n_seq
    npc = prows // crows
    nchunk = npc + 1
    nx = n_mp // 2
    back = min(-(-(LONGEST - 1) // crows), n_seq - 1)
    half = ROPE_BASE ** (-2.0 * np.arange(HALF, dtype=np.float64) / HD)
    freq = jnp.asarray(np.concatenate([half, half])[None, :], F32)
    cfg = (n_mp, n_seq, prows, crows, feat, qcols, kcols, ncomp)
    hbm = pl.BlockSpec(memory_space=pl.ANY)
    vmem = pl.BlockSpec(memory_space=pltpu.VMEM)
    dma = lambda *shape: pltpu.SemaphoreType.DMA(shape)
    rows = prows + crows
    z_hops = max(n_seq - 1, 1)
    results = pl.pallas_call(
        functools.partial(kernel, cfg),
        out_shape=(
            jax.ShapeDtypeStruct((prows, qcols), BF16),
            jax.ShapeDtypeStruct((n_seq * cap, qcols), BF16),
        ),
        in_specs=[hbm] * 5 + [vmem] * 3,
        out_specs=(vmem, vmem),
        scratch_shapes=[
            pltpu.VMEM((n_mp, rows, feat), BF16),
            pltpu.VMEM((depth, qcols), BF16),
            pltpu.VMEM((depth, kcols), BF16),
            pltpu.VMEM((depth, kcols), BF16),
            pltpu.VMEM((rows, HD), F32),
            pltpu.VMEM((rows, HD), F32),
            pltpu.VMEM((qcols // HD, rows, HD), BF16),
            pltpu.VMEM((n_seq, prows, 2 * kcols), BF16),
            pltpu.VMEM((back + 1, crows, 2 * kcols), BF16),
            pltpu.VMEM((n_seq * cap, crows), BF16),
            pltpu.VMEM((nkv, n_seq * cap, group * HD), BF16),
            pltpu.VMEM((qcols // HD, crows, HD), F32),
            pltpu.VMEM((qcols // HD, crows, HD), F32),
            pltpu.VMEM((qcols // HD, crows, HD), F32),
            dma(3),
            dma(nchunk),
            dma(nchunk, nx),
            dma(nchunk, 2 * nx - 1),
            dma(nchunk, nx - 1),
            dma(npc, z_hops), dma(npc, z_hops), dma(npc, z_hops), dma(npc, z_hops),
            dma(back), dma(back),
            dma(nkv, z_hops), dma(nkv, z_hops),
        ],
        compiler_params=pltpu.CompilerParams(
            collective_id=0, has_side_effects=True, vmem_limit_bytes=56 * 1024 * 1024
        ),
        cost_estimate=pl.CostEstimate(
            flops=2 * rows * depth * (qcols + 2 * kcols), bytes_accessed=2 * depth * (qcols + 2 * kcols), transcendentals=0
        ),
        name="grouped_attention",
    )(hidden_prompt, hidden_comp, w_query, w_key, w_value, lengths.reshape(1, ncomp), row_owner.reshape(1, crows), freq)
    return pl.pallas_call(
        hand_over,
        out_shape=tuple(jax.ShapeDtypeStruct(r.shape, BF16) for r in results),
        in_specs=[hbm] * 2,
        out_specs=(hbm, hbm),
        scratch_shapes=[pltpu.VMEM((2, max(prows, n_seq * cap), qcols), BF16), dma(2, PIECES), dma(2, PIECES)],
        name="hand_over",
    )(*results)


def solution(mesh):
    placed = (
        P(("groups", "seq"), "mp"),
        P(("groups", "seq"), "mp"),
        P(None, "mp"),
        P(None, "mp"),
        P(None, "mp"),
        P("groups"),
        P(("groups", "seq"), None),
    )
    return jax.shard_map(
        functools.partial(local, mesh.shape["mp"], mesh.shape["seq"]),
        mesh=mesh,
        in_specs=placed,
        out_specs=(P(("groups", "seq"), "mp"), P(("groups", "seq"), "mp")),
        check_vma=False,
    )
```
